32 devices in a mesh: seq: 8 (over z, y), kvh: 4 (over x, core).
Axes of the slice: x: 2, y: 2, z: 4, core: 2. Of those that a mesh axis runs over, the one named last changes fastest.
Arguments:
- queries: bfloat16 [512, 64, 128], P('seq', 'kvh'), may hold values from -15 to 15
- stretch_kv: bfloat16 [2, 512, 8, 128], P(None, 'seq', 'kvh'), may hold values from -15 to 15
- cache_kv: bfloat16 [2, 8, 2048, 8, 128], P(None, 'seq', None, 'kvh'), may hold values from -15 to 15
- selection: int32 [8, 512, 3], P('kvh', 'seq'), may hold values from 0 to 7, all different within a row; in each aligned block of 64 rows (0 to 63, 64 to 127, ..., all dimensions but the last counted through in order) at most 25 rows name the same one
- block_owner: int32 [8], replicated, may hold values from 0 to 7, each once
Outputs:
- attended: bfloat16 [512, 8192], P(('seq', 'kvh'))
The draws below stay inside these ranges and needn't reach their ends.
Inputs may be any that keep to these rules, and one draw needn't show every extreme that they name: `selection`: each KV head and token names 3 different blocks. Among the 64 tokens of one index of seq, for one KV head, no block is named more than 25 times, and some block is named exactly 25 times. `block_owner`: A permutation: each storage position holds exactly one block.
All inputs are finite; a program needn't handle non-finite values.
Results may differ from the reference program's by a relative error of at most 0.0051.
Values may be sent and summed in bfloat16 or wider, within the bound.
A program may use at most 128 MiB of HBM per device.

```python
import math
import jax
import jax.numpy as jnp
import numpy as np
from jax import lax

QUERY_HEAD_COUNT = 64
KEY_VALUE_HEADS = 8
HEAD_SIZE = 128
TOKENS_PER_SEQ = 64
BLOCK_TOKENS = 2048
PICKED_BLOCKS = 3
STRETCH_TOKENS = 512
CACHED_BLOCKS = 8
BLOCK_PICK_LIMIT = 25
CUR = 8
N_SEQ = 8


def coarse_field(key, shape):
    return jax.random.normal(jax.random.fold_in(key, 13), shape, jnp.float32)


def draw_queries(key, part):
    score_field = 2.0 * coarse_field(jax.random.fold_in(key, 1), (STRETCH_TOKENS, QUERY_HEAD_COUNT, HEAD_SIZE))
    return jnp.clip(score_field, -15.0, 15.0).astype(jnp.bfloat16)


def draw_stretch_kv(key, part):
    score_field = coarse_field(jax.random.fold_in(key, 2), (2, STRETCH_TOKENS, KEY_VALUE_HEADS, HEAD_SIZE))
    return jnp.clip(score_field, -15.0, 15.0).astype(jnp.bfloat16)


def draw_cache_kv(key, part):
    score_field = coarse_field(jax.random.fold_in(key, 3), (2, CACHED_BLOCKS, BLOCK_TOKENS, KEY_VALUE_HEADS, HEAD_SIZE))
    return jnp.clip(score_field, -15.0, 15.0).astype(jnp.bfloat16)


def routed_block(key, own, number, rows, number_of, top, limit, slope):
    sequence = jax.random.permutation(key, number_of)
    packed, common = shares(number_of, rows * top, limit, slope, True), shares(number_of, rows * top, limit, slope, False)
    places = jnp.arange(number_of)

    def named(tallies, offset_by):
        used = int((tallies > 0).sum())
        fixed = max(1, used // 4)
        shifted = fixed + (places - fixed + offset_by * (used - fixed)) % max(1, number_of - fixed)
        return jnp.zeros((number_of,), jnp.int32).at[sequence[jnp.where(places < fixed, places, shifted)]].set(jnp.asarray(tallies, jnp.int32))

    tallies = jnp.where(number % 4 == 0, named(packed, number // 4), named(common, number - number // 4 - 1))
    mixed = jax.random.permutation(jax.random.fold_in(own, 3), number_of)
    giver, receiver = mixed[0:number_of // 2 * 2:2], mixed[1:number_of // 2 * 2:2]
    room = jnp.minimum(tallies[giver] - 1, limit - tallies[receiver]) // 2
    room = jnp.where((giver == sequence[0]) | (receiver == sequence[0]) | (tallies[receiver] == 0), 0, jnp.maximum(room, 0))
    shifted = jax.random.randint(jax.random.fold_in(own, 4), (number_of // 2,), 0, 1 << 20) % (room + 1)
    tallies = tallies.at[giver].add(-shifted).at[receiver].add(shifted)
    members = jnp.searchsorted(jnp.cumsum(tallies), jnp.arange(rows * top), side="right").astype(jnp.int32)
    listing = members.reshape(top, rows).T
    listing = listing[jax.random.permutation(jax.random.fold_in(own, 1), rows)]
    offset_by = jax.random.randint(jax.random.fold_in(own, 2), (rows, 1), 0, top)
    return jnp.take_along_axis(listing, (jnp.arange(top)[None, :] + offset_by) % top, axis=1)


def shares(amount, total, most, skew, full):
    weights = [(1 << 20) // math.isqrt(rank ** skew) + 1 for rank in range(1, amount + 1)]
    largest = most if full else min(most, max(-(-total // amount), total * weights[0] // sum(weights)))
    least = 1 if total - largest >= amount - 1 else 0
    given, spare = [largest] + [least] * (amount - 1), total - largest - least * (amount - 1)
    while spare > 0:
        candidates = [i for i in range(1, amount) if given[i] < largest] or [i for i in range(1, amount) if given[i] < most]
        mass, remaining = sum([weights[i] for i in candidates]), spare
        for i in candidates:
            more = min(most - given[i], max(1, remaining * weights[i] // mass), spare)
            given[i] = given[i] + more
            spare = spare - more
    return np.array(given)


def setup_inputs(seed: int = 0) -> dict:
    splits = jax.random.split(jax.random.key(seed), 6)
    queries = draw_queries(jax.random.fold_in(splits[5], 71), 0)
    stretch_kv = draw_stretch_kv(jax.random.fold_in(splits[5], 71), 0)
    cache_kv = draw_cache_kv(jax.random.fold_in(splits[5], 71), 0)
    selection_keys = jax.random.split(jax.random.fold_in(splits[3], 1), KEY_VALUE_HEADS * STRETCH_TOKENS // TOKENS_PER_SEQ)
    selection_turns = jax.random.permutation(jax.random.fold_in(splits[3], 3), KEY_VALUE_HEADS * STRETCH_TOKENS // TOKENS_PER_SEQ)
    selection = jax.vmap(lambda own, number: routed_block(jax.random.fold_in(splits[3], 2), own, number, TOKENS_PER_SEQ, CACHED_BLOCKS, PICKED_BLOCKS, BLOCK_PICK_LIMIT, 2))(selection_keys, selection_turns).reshape((KEY_VALUE_HEADS, STRETCH_TOKENS, PICKED_BLOCKS))
    block_owner = jax.random.permutation(splits[4], CACHED_BLOCKS).astype(jnp.int32)
    return dict(queries=queries, stretch_kv=stretch_kv, cache_kv=cache_kv, selection=selection, block_owner=block_owner)


def reference(queries, stretch_kv, cache_kv, selection, block_owner):
    tokens_all, query_heads, head_dim = queries.shape
    kv_heads = stretch_kv.shape[2]
    group_size = query_heads // kv_heads
    scaling = 1.0 / math.sqrt(head_dim)
    piece_rows = TOKENS_PER_SEQ
    window_rows = CUR * piece_rows
    piece_count = tokens_all // piece_rows
    grouped = queries.reshape(tokens_all, kv_heads, group_size, head_dim)
    by_head = jnp.transpose(grouped, (1, 0, 2, 3))
    stretch_by_head = jnp.transpose(stretch_kv, (0, 2, 1, 3))
    padded_kv = jnp.pad(stretch_by_head, ((0, 0), (0, 0), ((CUR - 1) * piece_rows, 0), (0, 0)))
    anchor = jnp.int32(0)

    def current(index):
        kv_index = index // piece_count
        start = index % piece_count * piece_rows
        query_rows = lax.dynamic_slice(by_head, (kv_index, start, anchor, anchor), (1, piece_rows, group_size, head_dim))[0].astype(jnp.float32)
        stacked = lax.dynamic_slice(padded_kv, (anchor, kv_index, start, anchor), (2, 1, window_rows, head_dim))[:, 0].astype(jnp.float32)
        key_place = start - (CUR - 1) * piece_rows + jnp.arange(window_rows, dtype=jnp.int32)
        query_place = start + jnp.arange(piece_rows, dtype=jnp.int32)
        allowed = (key_place[None, :] >= 0) & (key_place[None, :] <= query_place[:, None])
        scores = jnp.einsum('tgd,kd->tgk', query_rows, stacked[0]) * scaling
        scores = jnp.where(allowed[:, None, :], scores, -jnp.inf)
        highest = lax.optimization_barrier(jnp.max(scores, axis=2))
        raw_weights = jnp.exp(scores - highest[..., None])
        weight_sum = lax.optimization_barrier(jnp.sum(raw_weights, axis=2))
        rounded = lax.optimization_barrier(raw_weights.astype(jnp.bfloat16)).astype(jnp.float32)
        blended = jnp.einsum('tgk,kd->tgd', rounded, stacked[1]) / weight_sum[..., None]
        return (blended, highest + jnp.log(weight_sum))
    cur_out, cur_lse = lax.map(current, jnp.arange(kv_heads * piece_count, dtype=jnp.int32))
    cur_out = jnp.transpose(cur_out.reshape(kv_heads, tokens_all, group_size, head_dim), (1, 0, 2, 3))
    cur_lse = jnp.transpose(cur_lse.reshape(kv_heads, tokens_all, group_size), (1, 0, 2))
    capacity = BLOCK_PICK_LIMIT * N_SEQ
    head_rows = jnp.arange(kv_heads, dtype=jnp.int32)[:, None]

    def visit(carry, block_id):
        running, log_total = carry
        holder = block_owner[block_id]
        stored = lax.dynamic_index_in_dim(cache_kv, holder, 1, keepdims=False).astype(jnp.float32)
        chosen = jnp.any(selection == block_id, axis=2)
        order = jnp.argsort(jnp.where(chosen, 0, 1), axis=1, stable=True)[:, :capacity].astype(jnp.int32)
        usable = jnp.take_along_axis(chosen, order, axis=1)
        query_rows = grouped[order, head_rows].astype(jnp.float32)
        scores = jnp.einsum('hcgd,khd->hcgk', query_rows, stored[0]) * scaling
        highest = lax.optimization_barrier(jnp.max(scores, axis=3))
        raw_weights = jnp.exp(scores - highest[..., None])
        weight_sum = lax.optimization_barrier(jnp.sum(raw_weights, axis=3))
        rounded = lax.optimization_barrier(raw_weights.astype(jnp.bfloat16)).astype(jnp.float32)
        blended = (jnp.einsum('hcgk,khd->hcgd', rounded, stored[1]) / weight_sum[..., None]).astype(jnp.bfloat16)
        block_lse = highest + jnp.log(weight_sum)
        old_lse = log_total[order, head_rows]
        old_mix = running[order, head_rows]
        new_lse = jnp.logaddexp(old_lse, block_lse)
        new_mix = old_mix * jnp.exp(old_lse - new_lse)[..., None] + blended.astype(jnp.float32) * jnp.exp(block_lse - new_lse)[..., None]
        keeping = usable[..., None]
        running = running.at[order, head_rows].set(jnp.where(keeping[..., None], new_mix, old_mix))
        log_total = log_total.at[order, head_rows].set(jnp.where(keeping, new_lse, old_lse))
        return ((running, log_total), None)
    (running, log_total), _ = lax.scan(visit, (cur_out, cur_lse), jnp.arange(CACHED_BLOCKS, dtype=jnp.int32))
    return running.astype(jnp.bfloat16).reshape(tokens_all, query_heads * head_dim)
```

```python
import functools
import math

import jax
import jax.numpy as jnp
from jax import lax
from jax.experimental import pallas as pl
from jax.experimental.pallas import tpu as pltpu
from jax.sharding import PartitionSpec as P

BLOCK_TOKENS = 2048
MESH = pl.DeviceIdType.MESH
LOW = -1e30


def iota(shape, axis):
    return lax.broadcasted_iota(jnp.int32, shape, axis)


def dot(a, b):
    return jnp.dot(a, b, preferred_element_type=jnp.float32)


def dot_nt(a, b):
    return lax.dot_general(a, b, (((1,), (1,)), ((), ())), preferred_element_type=jnp.float32)


def one_hot(hit):
    return jnp.where(hit, 1.0, 0.0).astype(jnp.bfloat16)


def kernel(
    cfg,
    sel_ref, inv_ref, q_ref, skv_ref, cache_ref,
    out_ref,
    raw, kd, vd, qp, val, valt, qout, qin, aout, ain, lout, lin, st, m_ref, l_ref, acc, fin,
    load_sem, qs_sem, qr_sem, as_sem, ar_sem, ls_sem, lr_sem, ss_sem, sr_sem, fs_sem, fr_sem,
):
    N, KVH, KV, G, T, D, C, RP, RL, W, KEYS = cfg
    H = KV * G
    GT = G * T
    scale = 1.0 / math.sqrt(D)
    me = lax.axis_index("seq")
    mk = lax.axis_index("kvh")
    load = pltpu.make_async_copy(cache_ref, raw, load_sem)
    load.start()

    barrier = pltpu.get_barrier_semaphore()

    def greet(o, carry):
        pl.semaphore_signal(barrier, inc=1, device_id=(lax.rem(me + o, N), mk), device_id_type=MESH)
        return carry

    lax.fori_loop(1, N, greet, 0)

    def greet_kvh(o, carry):
        pl.semaphore_signal(barrier, inc=1, device_id=(me, lax.rem(mk + o, KVH)), device_id_type=MESH)
        return carry

    lax.fori_loop(1, KVH, greet_kvh, 0)

    tb = 256 // H
    r, c = iota((256, 256), 0), iota((256, 256), 1)
    order = one_hot(c == (r % tb) * H + r // tb)
    for b in range(T // tb):
        moved = dot(order, q_ref[b * 256:(b + 1) * 256, :]).astype(jnp.bfloat16)
        for h in range(H):
            qp[h // G, (h % G) * T + b * tb:(h % G) * T + (b + 1) * tb, :] = moved[h * tb:(h + 1) * tb]

    upper = one_hot(iota((T, T), 0) <= iota((T, T), 1))
    spread = one_hot(iota((T, GT), 0) == iota((T, GT), 1) % T)
    group = iota((N, GT), 1) // T
    for kv in range(KV):
        hit = inv_ref[...] == sel_ref[kv, 0:1, :]
        for k in range(1, sel_ref.shape[1]):
            hit = jnp.logical_or(hit, inv_ref[...] == sel_ref[kv, k:k + 1, :])
        rank = jnp.where(hit, dot(one_hot(hit), upper), 0.0)
        wide = dot(rank.astype(jnp.bfloat16), spread).astype(jnp.int32)
        rows = jnp.where(wide > 0, (wide - 1) * G + group, -1)
        val[kv] = rows
        padded = rows.astype(jnp.float32)
        if N < 128:
            padded = jnp.concatenate([padded, jnp.zeros((128 - N, GT), jnp.float32)], axis=0)
        valt[kv] = jnp.transpose(padded)

    pl.semaphore_wait(barrier, N - 1 + KVH - 1)

    def piece(s):
        return pltpu.make_async_remote_copy(
            src_ref=st.at[s], dst_ref=st.at[s + 1], send_sem=ss_sem.at[s], recv_sem=sr_sem.at[s + 1],
            device_id=(lax.rem(me + 1, N), mk), device_id_type=MESH,
        )

    def first_piece():
        return pltpu.make_async_remote_copy(
            src_ref=skv_ref, dst_ref=st.at[1], send_sem=ss_sem.at[0], recv_sem=sr_sem.at[1],
            device_id=(lax.rem(me + 1, N), mk), device_id_type=MESH,
        )

    def query(o, kv):
        return pltpu.make_async_remote_copy(
            src_ref=qout.at[o, kv], dst_ref=qin.at[o, kv], send_sem=qs_sem.at[o, kv],
            recv_sem=qr_sem.at[o, kv], device_id=(lax.rem(me + o, N), mk), device_id_type=MESH,
        )

    def answer(o, kv):
        return pltpu.make_async_remote_copy(
            src_ref=aout.at[o, kv], dst_ref=ain.at[o, kv], send_sem=as_sem.at[o, kv],
            recv_sem=ar_sem.at[o, kv], device_id=(lax.rem(me + N - o, N), mk), device_id_type=MESH,
        )

    def answer_lse(o):
        return pltpu.make_async_remote_copy(
            src_ref=lout.at[o], dst_ref=lin.at[o], send_sem=ls_sem.at[o],
            recv_sem=lr_sem.at[o], device_id=(lax.rem(me + N - o, N), mk), device_id_type=MESH,
        )

    if W > 1:
        @pl.when(me + 1 < N)
        def _():
            first_piece().start()

    def packed(o, kv):
        line = val[kv, pl.ds(lax.rem(me + o, N), 1), :]
        pick = one_hot(iota((RP, GT), 0) == line)
        return dot(pick, qp[kv]).astype(jnp.bfloat16)

    def send(o, carry):
        for kv in range(KV):
            qout[o, kv] = packed(o, kv)
            query(o, kv).start()
        return carry

    lax.fori_loop(1, N, send, 0)
    for kv in range(KV):
        qin[0, kv] = packed(0, kv)

    load.wait()
    split = one_hot(c == (r % (256 // KV)) * KV + r // (256 // KV))
    per = 256 // KV

    def unmix(b, carry):
        src = pl.ds(pl.multiple_of(b * 256, 256), 256)
        dst = pl.ds(pl.multiple_of(b * per, per), per)
        keys = dot(split, raw[0, src, :]).astype(jnp.bfloat16)
        values = dot(split, raw[1, src, :]).astype(jnp.bfloat16)
        for kv in range(KV):
            kd[kv, dst, :] = keys[kv * per:(kv + 1) * per]
            vd[kv, dst, :] = values[kv * per:(kv + 1) * per]
        return carry

    lax.fori_loop(0, KEYS * KV // 256, unmix, 0)

    def absorb(keys, values, causal):
        row, col = iota((GT, T * KV), 0), iota((GT, T * KV), 1)
        for kv in range(KV):
            allowed = col % KV == kv
            if causal:
                allowed = jnp.logical_and(allowed, col // KV <= row % T)
            s = jnp.where(allowed, dot_nt(qp[kv], keys) * scale, LOW)
            top = jnp.max(s, axis=1, keepdims=True)
            if causal:
                p = jnp.exp(s - top)
                m_ref[kv] = top
                l_ref[kv] = jnp.sum(p, axis=1, keepdims=True)
                acc[kv] = dot(p.astype(jnp.bfloat16), values)
            else:
                new = jnp.maximum(m_ref[kv], top)
                fade = jnp.exp(m_ref[kv] - new)
                p = jnp.exp(s - new)
                m_ref[kv] = new
                l_ref[kv] = l_ref[kv] * fade + jnp.sum(p, axis=1, keepdims=True)
                acc[kv] = acc[kv] * fade + dot(p.astype(jnp.bfloat16), values)

    absorb(skv_ref[0], skv_ref[1], True)

    def serve(o):
        for kv in range(KV):
            @pl.when(o > 0)
            def _():
                query(o, kv).wait_recv()
            s = dot_nt(qin[o, kv], kd[kv])
            top = jnp.max(s, axis=1, keepdims=True)
            p = jnp.exp((s - top) * scale)
            total = jnp.sum(p, axis=1, keepdims=True)
            res = (dot(p.astype(jnp.bfloat16), vd[kv]) / total).astype(jnp.bfloat16)
            lse = top * scale + jnp.log(total)
            flat = jnp.broadcast_to(lse, (RP, 128))
            if RL > RP:
                flat = jnp.concatenate([flat, jnp.zeros((RL - RP, 128), jnp.float32)], axis=0)
            line = jnp.transpose(flat)[0:1, :]

            @pl.when(o > 0)
            def _():
                aout[o, kv] = res
                lout[o, kv:kv + 1, :] = line
                answer(o, kv).start()

            @pl.when(o == 0)
            def _():
                ain[0, kv] = res
                lin[0, kv:kv + 1, :] = line

        @pl.when(o > 0)
        def _():
            answer_lse(o).start()

    def turn(o, carry):
        @pl.when(jnp.logical_and(o < W, jnp.logical_and(o > 0, o <= me)))
        def _():
            piece(o - 1).wait_recv()

            @pl.when(jnp.logical_and(o + 1 < W, me + 1 < N))
            def _():
                piece(o).start()

            absorb(st[o, 0], st[o, 1], False)

        serve(o)
        return carry

    lax.fori_loop(0, N, turn, 0)

    lane = iota((GT, 128), 1)
    slot = iota((GT, RL), 1)

    def merge(o, carry):
        @pl.when(o > 0)
        def _():
            answer_lse(o).wait_recv()

        dest = lax.rem(me + o, N)
        for kv in range(KV):
            @pl.when(o > 0)
            def _():
                answer(o, kv).wait_recv()
            mine = jnp.sum(jnp.where(lane == dest, valt[kv], 0.0), axis=1, keepdims=True).astype(jnp.int32)
            hit = slot == mine
            lse = jnp.sum(jnp.where(hit, lin[o, kv:kv + 1, :], 0.0), axis=1, keepdims=True)
            lse = jnp.where(mine >= 0, lse, LOW)
            got = dot(one_hot(hit[:, :RP]), ain[o, kv])
            new = jnp.maximum(m_ref[kv], lse)
            fade = jnp.exp(m_ref[kv] - new)
            w = jnp.exp(lse - new)
            m_ref[kv] = new
            l_ref[kv] = l_ref[kv] * fade + w
            acc[kv] = acc[kv] * fade + got * w
        return carry

    lax.fori_loop(0, N, merge, 0)

    for kv in range(KV):
        whole = (acc[kv] / l_ref[kv]).astype(jnp.bfloat16)
        for g in range(G):
            fin[:, (kv * G + g) * D:(kv * G + g + 1) * D] = whole[g * T:(g + 1) * T]

    TO = T // KVH
    HD = H * D
    columns = pl.ds(pl.multiple_of(mk * HD, HD), HD)

    def part(j):
        to = lax.rem(mk + j, KVH)
        return pltpu.make_async_remote_copy(
            src_ref=fin.at[pl.ds(pl.multiple_of(to * TO, TO), TO), :], dst_ref=out_ref.at[:, columns],
            send_sem=fs_sem.at[j], recv_sem=fr_sem.at[j], device_id=(me, to), device_id_type=MESH,
        )

    for j in range(1, KVH):
        part(j).start()
    own = pltpu.make_async_copy(
        fin.at[pl.ds(pl.multiple_of(mk * TO, TO), TO), :], out_ref.at[:, columns], load_sem
    )
    own.start()

    def drain(o, carry):
        for kv in range(KV):
            query(o, kv).wait_send()
            answer(o, kv).wait_send()
        answer_lse(o).wait_send()
        return carry

    lax.fori_loop(1, N, drain, 0)
    if W > 1:
        @pl.when(me + 1 < N)
        def _():
            first_piece().wait_send()

    def drain_piece(o, carry):
        @pl.when(jnp.logical_and(o <= me, me + 1 < N))
        def _():
            piece(o).wait_send()
        return carry

    lax.fori_loop(1, W - 1, drain_piece, 0)
    own.wait()
    for j in range(1, KVH):
        part(j).wait()


def per_device(queries, stretch_kv, cache_kv, selection, block_owner):
    T, H, D = queries.shape
    KV = stretch_kv.shape[2]
    G = H // KV
    top = selection.shape[2]
    N = lax.axis_size("seq")
    KVH = lax.axis_size("kvh")
    C = max(2, top * T // N + 1)
    RP = -(-C * G // 16) * 16
    RL = -(-RP // 128) * 128
    W = min(BLOCK_TOKENS // T, N)
    KEYS = cache_kv.shape[2]
    cfg = (N, KVH, KV, G, T, D, C, RP, RL, W, KEYS)
    places = jnp.arange(N, dtype=jnp.int32)
    inverse = jnp.sum(
        jnp.where(block_owner[None, :] == places[:, None], places[None, :], 0), axis=1, keepdims=True
    )
    bf, f32 = jnp.bfloat16, jnp.float32
    vm = pl.BlockSpec(memory_space=pltpu.VMEM)
    dma = pltpu.SemaphoreType.DMA
    return pl.pallas_call(
        functools.partial(kernel, cfg),
        out_shape=jax.ShapeDtypeStruct((T // KVH, KVH * H * D), bf),
        in_specs=[vm, vm, vm, vm, pl.BlockSpec(memory_space=pl.ANY)],
        out_specs=vm,
        scratch_shapes=[
            pltpu.VMEM((2, KEYS * KV, D), bf),
            pltpu.VMEM((KV, KEYS, D), bf),
            pltpu.VMEM((KV, KEYS, D), bf),
            pltpu.VMEM((KV, G * T, D), bf),
            pltpu.VMEM((KV, N, G * T), jnp.int32),
            pltpu.VMEM((KV, G * T, 128), f32),
            pltpu.VMEM((N, KV, RP, D), bf),
            pltpu.VMEM((N, KV, RP, D), bf),
            pltpu.VMEM((N, KV, RP, D), bf),
            pltpu.VMEM((N, KV, RP, D), bf),
            pltpu.VMEM((N, 8, RL), f32),
            pltpu.VMEM((N, 8, RL), f32),
            pltpu.VMEM((W, 2, T * KV, D), bf),
            pltpu.VMEM((KV, G * T, 1), f32),
            pltpu.VMEM((KV, G * T, 1), f32),
            pltpu.VMEM((KV, G * T, D), f32),
            pltpu.VMEM((T, H * D), bf),
            dma, dma((N, KV)), dma((N, KV)), dma((N, KV)), dma((N, KV)), dma((N,)), dma((N,)),
            dma((W,)), dma((W,)), dma((KVH,)), dma((KVH,)),
        ],
        compiler_params=pltpu.CompilerParams(
            collective_id=0, has_side_effects=True, vmem_limit_bytes=56 * 1024 * 1024
        ),
        cost_estimate=pl.CostEstimate(
            flops=4 * N * RP * KV * KEYS * D, bytes_accessed=4 * KEYS * KV * D, transcendentals=N * RP * KV * KEYS
        ),
    )(
        jnp.swapaxes(selection, 1, 2),
        inverse,
        queries.reshape(T * H, D),
        stretch_kv.reshape(2, T * KV, D),
        cache_kv.reshape(2, KEYS * KV, D),
    )


def solution(mesh):
    placed = (
        P("seq", "kvh", None),
        P(None, "seq", "kvh", None),
        P(None, "seq", None, "kvh", None),
        P("kvh", "seq", None),
        P(),
    )
    return jax.shard_map(
        per_device, mesh=mesh, in_specs=placed, out_specs=P(("seq", "kvh"), None), check_vma=False
    )
```

```python
import functools
import math

import jax
import jax.numpy as jnp
from jax import lax
from jax.experimental import pallas as pl
from jax.experimental.pallas import tpu as pltpu
from jax.sharding import PartitionSpec as P

BLOCK_TOKENS = 2048
MESH = pl.DeviceIdType.MESH
LOW = -1e30
LOG2E = math.log2(math.e)


def iota(shape, axis):
    return lax.broadcasted_iota(jnp.int32, shape, axis)


def dot(a, b):
    return jnp.dot(a, b, preferred_element_type=jnp.float32)


def dot_nt(a, b):
    return lax.dot_general(a, b, (((1,), (1,)), ((), ())), preferred_element_type=jnp.float32)


def one_hot(hit):
    return jnp.where(hit, 1.0, 0.0).astype(jnp.bfloat16)


def kernel(
    cfg,
    sel_ref, owner_ref, q_ref, skv_ref, cache_ref,
    out_ref,
    raw, kd, vd, qp, val, valt, qout, qin, aout, ain, lout, lin, st, sk, sv, m_ref, l_ref, acc, fin,
    load_sem, qs_sem, qr_sem, as_sem, ar_sem, ls_sem, lr_sem, ss_sem, sr_sem, fs_sem, fr_sem,
):
    N, KVH, KV, G, T, D, C, RP, RL, W, KEYS = cfg
    H = KV * G
    GT = G * T
    scale = 1.0 / math.sqrt(D)
    me = lax.axis_index("seq")
    mk = lax.axis_index("kvh")
    load = pltpu.make_async_copy(cache_ref, raw, load_sem)
    load.start()

    barrier = pltpu.get_barrier_semaphore()

    def greet(o, carry):
        pl.semaphore_signal(barrier, inc=1, device_id=(lax.rem(me + o, N), mk), device_id_type=MESH)
        return carry

    lax.fori_loop(1, N, greet, 0)

    def greet_kvh(o, carry):
        pl.semaphore_signal(barrier, inc=1, device_id=(me, lax.rem(mk + o, KVH)), device_id_type=MESH)
        return carry

    lax.fori_loop(1, KVH, greet_kvh, 0)

    tb = 256 // H
    r, c = iota((256, 256), 0), iota((256, 256), 1)
    order = one_hot(c == (r % tb) * H + r // tb)
    for b in range(T // tb):
        moved = dot(order, q_ref[b * 256:(b + 1) * 256, :]).astype(jnp.bfloat16)
        for h in range(H):
            qp[h // G, (h % G) * T + b * tb:(h % G) * T + (b + 1) * tb, :] = moved[h * tb:(h + 1) * tb]

    upper = one_hot(iota((T, T), 0) <= iota((T, T), 1))
    same = one_hot(iota((T, T), 0) == iota((T, T), 1))
    spread = one_hot(iota((T, GT), 0) == iota((T, GT), 1) % T)
    group = iota((N, GT), 1) // T
    owns = one_hot(iota((N, N), 0) == owner_ref[...])
    for kv in range(KV):
        named = iota((T, N), 1) == sel_ref[kv, :, 0:1]
        for k in range(1, sel_ref.shape[2]):
            named = jnp.logical_or(named, iota((T, N), 1) == sel_ref[kv, :, k:k + 1])
        named = dot_nt(owns, one_hot(named)).astype(jnp.bfloat16)
        rank = dot(named, upper) * dot(named, same)
        wide = dot(rank.astype(jnp.bfloat16), spread).astype(jnp.int32)
        rows = jnp.where(wide > 0, (wide - 1) * G + group, -1)
        val[kv] = rows
        padded = rows.astype(jnp.float32)
        if N < 128:
            padded = jnp.concatenate([padded, jnp.zeros((128 - N, GT), jnp.float32)], axis=0)
        valt[kv] = jnp.transpose(padded)

    pl.semaphore_wait(barrier, N - 1 + KVH - 1)

    def piece(s):
        return pltpu.make_async_remote_copy(
            src_ref=st.at[s], dst_ref=st.at[s + 1], send_sem=ss_sem.at[s], recv_sem=sr_sem.at[s + 1],
            device_id=(lax.rem(me + 1, N), mk), device_id_type=MESH,
        )

    def first_piece():
        return pltpu.make_async_remote_copy(
            src_ref=skv_ref, dst_ref=st.at[1], send_sem=ss_sem.at[0], recv_sem=sr_sem.at[1],
            device_id=(lax.rem(me + 1, N), mk), device_id_type=MESH,
        )

    def query(o):
        return pltpu.make_async_remote_copy(
            src_ref=qout.at[o], dst_ref=qin.at[o], send_sem=qs_sem.at[o],
            recv_sem=qr_sem.at[o], device_id=(lax.rem(me + o, N), mk), device_id_type=MESH,
        )

    def answer(o):
        return pltpu.make_async_remote_copy(
            src_ref=aout.at[o], dst_ref=ain.at[o], send_sem=as_sem.at[o],
            recv_sem=ar_sem.at[o], device_id=(lax.rem(me + N - o, N), mk), device_id_type=MESH,
        )

    def answer_lse(o):
        return pltpu.make_async_remote_copy(
            src_ref=lout.at[o], dst_ref=lin.at[o], send_sem=ls_sem.at[o],
            recv_sem=lr_sem.at[o], device_id=(lax.rem(me + N - o, N), mk), device_id_type=MESH,
        )

    if W > 1:
        @pl.when(me + 1 < N)
        def _():
            first_piece().start()

    def packed(o, kv):
        line = val[kv, pl.ds(lax.rem(me + o, N), 1), :]
        pick = one_hot(iota((RP, GT), 0) == line)
        return dot(pick, qp[kv]).astype(jnp.bfloat16)

    def send(o, carry):
        for kv in range(KV):
            qout[o, kv] = packed(o, kv)
        query(o).start()
        return carry

    lax.fori_loop(1, N, send, 0)
    for kv in range(KV):
        qin[0, kv] = packed(0, kv)

    load.wait()
    split = one_hot(c == (r % (256 // KV)) * KV + r // (256 // KV))
    per = 256 // KV

    def unmix(b, carry):
        src = pl.ds(pl.multiple_of(b * 256, 256), 256)
        dst = pl.ds(pl.multiple_of(b * per, per), per)
        keys = dot(split, raw[0, src, :]).astype(jnp.bfloat16)
        values = dot(split, raw[1, src, :]).astype(jnp.bfloat16)
        for kv in range(KV):
            kd[kv, dst, :] = keys[kv * per:(kv + 1) * per]
            vd[kv, dst, 0:D] = values[kv * per:(kv + 1) * per]
            vd[kv, dst, D:2 * D] = jnp.ones((per, D), jnp.bfloat16)
        return carry

    lax.fori_loop(0, KEYS * KV // 256, unmix, 0)

    def serve(o, answers, lines):
        for kv in range(KV):
            s = dot_nt(qin[o, kv], kd[kv])
            top = jnp.max(s, axis=1, keepdims=True)
            p = jnp.exp2((s - top) * (scale * LOG2E)).astype(jnp.bfloat16)
            res = dot(p, vd[kv])
            total = res[:, D:2 * D]
            answers[o, kv] = (res[:, 0:D] / total).astype(jnp.bfloat16)
            flat = top * scale + jnp.log(total)
            if RL > RP:
                flat = jnp.concatenate([flat, jnp.zeros((RL - RP, D), jnp.float32)], axis=0)
            lines[o, kv:kv + 1, :] = jnp.transpose(flat)[0:1, :]

    def blank(o, carry):
        st[o] = jnp.zeros((2, T * KV, D), jnp.bfloat16)
        return carry

    st[0] = skv_ref[...]
    lax.fori_loop(me + 1, W, blank, 0)
    serve(0, ain, lin)

    def turn(o, carry):
        @pl.when(jnp.logical_and(o < W, o <= me))
        def _():
            piece(o - 1).wait_recv()

            @pl.when(jnp.logical_and(o + 1 < W, me + 1 < N))
            def _():
                piece(o).start()

        query(o).wait_recv()
        serve(o, aout, lout)
        answer(o).start()
        answer_lse(o).start()
        return carry

    lax.fori_loop(1, N, turn, 0)

    pt = 256 // (T * KV)
    c2 = iota((256, 256), 1)
    r2 = iota((256, 256), 0)
    apart = one_hot(c2 == (r2 % (pt * T)) * KV + r2 // (pt * T))
    for b in range(W // pt):
        keys = dot(apart, st[b * pt:(b + 1) * pt, 0].reshape(256, D)).astype(jnp.bfloat16)
        values = dot(apart, st[b * pt:(b + 1) * pt, 1].reshape(256, D)).astype(jnp.bfloat16)
        for kv in range(KV):
            sk[kv, b * pt * T:(b + 1) * pt * T, :] = keys[kv * pt * T:(kv + 1) * pt * T]
            sv[kv, b * pt * T:(b + 1) * pt * T, 0:D] = values[kv * pt * T:(kv + 1) * pt * T]
            sv[kv, b * pt * T:(b + 1) * pt * T, D:2 * D] = jnp.ones((pt * T, D), jnp.bfloat16)
    row, col = iota((GT, W * T), 0), iota((GT, W * T), 1)
    allowed = jnp.logical_and(col < (me + 1) * T, col <= row % T + jnp.where(col < T, 0, W * T))
    for kv in range(KV):
        s = jnp.where(allowed, dot_nt(qp[kv], sk[kv]), LOW)
        top = jnp.max(s, axis=1, keepdims=True)
        p = jnp.exp2((s - top) * (scale * LOG2E)).astype(jnp.bfloat16)
        res = dot(p, sv[kv])
        m_ref[kv] = top * scale
        l_ref[kv] = res[:, D:D + 1]
        acc[kv] = res[:, 0:D]

    lane = iota((GT, 128), 1)
    slot = iota((GT, RL), 1)

    def merge(o, carry):
        @pl.when(o > 0)
        def _():
            answer(o).wait_recv()
            answer_lse(o).wait_recv()

        dest = lax.rem(me + o, N)
        for kv in range(KV):
            mine = jnp.sum(jnp.where(lane == dest, valt[kv], 0.0), axis=1, keepdims=True).astype(jnp.int32)
            hit = slot == mine
            lse = jnp.sum(jnp.where(hit, lin[o, kv:kv + 1, :], 0.0), axis=1, keepdims=True)
            lse = jnp.where(mine >= 0, lse, LOW)
            got = dot(one_hot(hit[:, :RP]), ain[o, kv])
            new = jnp.maximum(m_ref[kv], lse)
            fade = jnp.exp(m_ref[kv] - new)
            w = jnp.exp(lse - new)
            m_ref[kv] = new
            l_ref[kv] = l_ref[kv] * fade + w
            acc[kv] = acc[kv] * fade + got * w
        return carry

    lax.fori_loop(0, N, merge, 0)

    for kv in range(KV):
        whole = (acc[kv] / l_ref[kv]).astype(jnp.bfloat16)
        for g in range(G):
            fin[:, (kv * G + g) * D:(kv * G + g + 1) * D] = whole[g * T:(g + 1) * T]

    TO = T // KVH
    HD = H * D
    columns = pl.ds(pl.multiple_of(mk * HD, HD), HD)

    def part(j):
        to = lax.rem(mk + j, KVH)
        return pltpu.make_async_remote_copy(
            src_ref=fin.at[pl.ds(pl.multiple_of(to * TO, TO), TO), :], dst_ref=out_ref.at[:, columns],
            send_sem=fs_sem.at[j], recv_sem=fr_sem.at[j], device_id=(me, to), device_id_type=MESH,
        )

    for j in range(1, KVH):
        part(j).start()
    own = pltpu.make_async_copy(
        fin.at[pl.ds(pl.multiple_of(mk * TO, TO), TO), :], out_ref.at[:, columns], load_sem
    )
    own.start()

    def drain(o, carry):
        query(o).wait_send()
        answer(o).wait_send()
        answer_lse(o).wait_send()
        return carry

    lax.fori_loop(1, N, drain, 0)
    if W > 1:
        @pl.when(me + 1 < N)
        def _():
            first_piece().wait_send()

    def drain_piece(o, carry):
        @pl.when(jnp.logical_and(o <= me, me + 1 < N))
        def _():
            piece(o).wait_send()
        return carry

    lax.fori_loop(1, W - 1, drain_piece, 0)
    own.wait()
    for j in range(1, KVH):
        part(j).wait()


def per_device(queries, stretch_kv, cache_kv, selection, block_owner):
    T, H, D = queries.shape
    KV = stretch_kv.shape[2]
    G = H // KV
    top = selection.shape[2]
    N = lax.axis_size("seq")
    KVH = lax.axis_size("kvh")
    C = max(2, top * T // N + 1)
    RP = -(-C * G // 16) * 16
    RL = -(-RP // 128) * 128
    W = min(BLOCK_TOKENS // T, N)
    KEYS = cache_kv.shape[2]
    cfg = (N, KVH, KV, G, T, D, C, RP, RL, W, KEYS)
    bf, f32 = jnp.bfloat16, jnp.float32
    vm = pl.BlockSpec(memory_space=pltpu.VMEM)
    dma = pltpu.SemaphoreType.DMA
    return pl.pallas_call(
        functools.partial(kernel, cfg),
        out_shape=jax.ShapeDtypeStruct((T // KVH, KVH * H * D), bf),
        in_specs=[vm, vm, vm, vm, pl.BlockSpec(memory_space=pl.ANY)],
        out_specs=vm,
        scratch_shapes=[
            pltpu.VMEM((2, KEYS * KV, D), bf),
            pltpu.VMEM((KV, KEYS, D), bf),
            pltpu.VMEM((KV, KEYS, 2 * D), bf),
            pltpu.VMEM((KV, G * T, D), bf),
            pltpu.VMEM((KV, N, G * T), jnp.int32),
            pltpu.VMEM((KV, G * T, 128), f32),
            pltpu.VMEM((N, KV, RP, D), bf),
            pltpu.VMEM((N, KV, RP, D), bf),
            pltpu.VMEM((N, KV, RP, D), bf),
            pltpu.VMEM((N, KV, RP, D), bf),
            pltpu.VMEM((N, 8, RL), f32),
            pltpu.VMEM((N, 8, RL), f32),
            pltpu.VMEM((W, 2, T * KV, D), bf),
            pltpu.VMEM((KV, W * T, D), bf),
            pltpu.VMEM((KV, W * T, 2 * D), bf),
            pltpu.VMEM((KV, G * T, 1), f32),
            pltpu.VMEM((KV, G * T, 1), f32),
            pltpu.VMEM((KV, G * T, D), f32),
            pltpu.VMEM((T, H * D), bf),
            dma, dma((N,)), dma((N,)), dma((N,)), dma((N,)), dma((N,)), dma((N,)),
            dma((W,)), dma((W,)), dma((KVH,)), dma((KVH,)),
        ],
        compiler_params=pltpu.CompilerParams(
            collective_id=0, has_side_effects=True, vmem_limit_bytes=56 * 1024 * 1024
        ),
        cost_estimate=pl.CostEstimate(
            flops=4 * N * RP * KV * KEYS * D, bytes_accessed=4 * KEYS * KV * D, transcendentals=N * RP * KV * KEYS
        ),
    )(
        selection,
        block_owner.reshape(1, N),
        queries.reshape(T * H, D),
        stretch_kv.reshape(2, T * KV, D),
        cache_kv.reshape(2, KEYS * KV, D),
    )


def solution(mesh):
    placed = (
        P("seq", "kvh", None),
        P(None, "seq", "kvh", None),
        P(None, "seq", None, "kvh", None),
        P("kvh", "seq", None),
        P(),
    )
    return jax.shard_map(
        per_device, mesh=mesh, in_specs=placed, out_specs=P(("seq", "kvh"), None), check_vma=False
    )
```

```python
import functools
import math

import jax
import jax.numpy as jnp
from jax import lax
from jax.experimental import pallas as pl
from jax.experimental.pallas import tpu as pltpu
from jax.sharding import PartitionSpec as P

BLOCK_TOKENS = 2048
MESH = pl.DeviceIdType.MESH
LOW = -1e30
LOG2E = math.log2(math.e)


def iota(shape, axis):
    return lax.broadcasted_iota(jnp.int32, shape, axis)


def dot(a, b):
    return jnp.dot(a, b, preferred_element_type=jnp.float32)


def dot_nt(a, b):
    return lax.dot_general(a, b, (((1,), (1,)), ((), ())), preferred_element_type=jnp.float32)


def one_hot(hit):
    return jnp.where(hit, 1.0, 0.0).astype(jnp.bfloat16)


def kernel(
    cfg,
    sel_ref, owner_ref, q_ref, skv_ref, cache_ref,
    out_ref,
    raw, kd, vd, qp, val, valt, qout, qin, aout, ain, lout, lin, st, sk, sv, m_ref, l_ref, acc, fin,
    load_sem, qs_sem, qr_sem, as_sem, ar_sem, ls_sem, lr_sem, ss_sem, sr_sem, fs_sem, fr_sem,
):
    N, KVH, KV, G, T, D, C, RP, RL, W, KEYS = cfg
    H = KV * G
    GT = G * T
    scale = 1.0 / math.sqrt(D)
    me = lax.axis_index("seq")
    mk = lax.axis_index("kvh")
    load = pltpu.make_async_copy(cache_ref, raw, load_sem)
    load.start()

    barrier = pltpu.get_barrier_semaphore()

    def greet(o, carry):
        pl.semaphore_signal(barrier, inc=1, device_id=(lax.rem(me + o, N), mk), device_id_type=MESH)
        return carry

    lax.fori_loop(1, N, greet, 0)

    def greet_kvh(o, carry):
        pl.semaphore_signal(barrier, inc=1, device_id=(me, lax.rem(mk + o, KVH)), device_id_type=MESH)
        return carry

    lax.fori_loop(1, KVH, greet_kvh, 0)

    tb = 256 // H
    r, c = iota((256, 256), 0), iota((256, 256), 1)
    order = one_hot(c == (r % tb) * H + r // tb)
    for b in range(T // tb):
        moved = dot(order, q_ref[b * 256:(b + 1) * 256, :]).astype(jnp.bfloat16)
        for h in range(H):
            qp[h // G, (h % G) * T + b * tb:(h % G) * T + (b + 1) * tb, :] = moved[h * tb:(h + 1) * tb]

    upper = one_hot(iota((T, T), 0) <= iota((T, T), 1))
    same = one_hot(iota((T, T), 0) == iota((T, T), 1))
    spread = one_hot(iota((T, GT), 0) == iota((T, GT), 1) % T)
    group = iota((N, GT), 1) // T
    owns = one_hot(iota((N, N), 0) == owner_ref[...])
    for kv in range(KV):
        named = iota((T, N), 1) == sel_ref[kv, :, 0:1]
        for k in range(1, sel_ref.shape[2]):
            named = jnp.logical_or(named, iota((T, N), 1) == sel_ref[kv, :, k:k + 1])
        named = dot_nt(owns, one_hot(named)).astype(jnp.bfloat16)
        rank = dot(named, upper) * dot(named, same)
        wide = dot(rank.astype(jnp.bfloat16), spread).astype(jnp.int32)
        rows = jnp.where(wide > 0, (wide - 1) * G + group, -1)
        val[kv] = rows
        padded = rows.astype(jnp.float32)
        if N < 128:
            padded = jnp.concatenate([padded, jnp.zeros((128 - N, GT), jnp.float32)], axis=0)
        valt[kv] = jnp.transpose(padded).astype(jnp.bfloat16)

    def packed(o, kv):
        line = val[kv, pl.ds(lax.rem(me + o, N), 1), :]
        pick = one_hot(iota((RP, GT), 0) == line)
        return dot(pick, qp[kv]).astype(jnp.bfloat16)

    def pack(o, carry):
        for kv in range(KV):
            qout[o, kv] = packed(o, kv)
        return carry

    lax.fori_loop(1, N, pack, 0)
    pl.semaphore_wait(barrier, N - 1 + KVH - 1)

    def piece(s):
        return pltpu.make_async_remote_copy(
            src_ref=st.at[s], dst_ref=st.at[s + 1], send_sem=ss_sem.at[s], recv_sem=sr_sem.at[s + 1],
            device_id=(lax.rem(me + 1, N), mk), device_id_type=MESH,
        )

    def first_piece():
        return pltpu.make_async_remote_copy(
            src_ref=skv_ref, dst_ref=st.at[1], send_sem=ss_sem.at[0], recv_sem=sr_sem.at[1],
            device_id=(lax.rem(me + 1, N), mk), device_id_type=MESH,
        )

    def query(o):
        return pltpu.make_async_remote_copy(
            src_ref=qout.at[o], dst_ref=qin.at[o], send_sem=qs_sem.at[o],
            recv_sem=qr_sem.at[o], device_id=(lax.rem(me + o, N), mk), device_id_type=MESH,
        )

    def answer(o):
        return pltpu.make_async_remote_copy(
            src_ref=aout.at[o], dst_ref=ain.at[o], send_sem=as_sem.at[o],
            recv_sem=ar_sem.at[o], device_id=(lax.rem(me + N - o, N), mk), device_id_type=MESH,
        )

    def answer_lse(o):
        return pltpu.make_async_remote_copy(
            src_ref=lout.at[o], dst_ref=lin.at[o], send_sem=ls_sem.at[o],
            recv_sem=lr_sem.at[o], device_id=(lax.rem(me + N - o, N), mk), device_id_type=MESH,
        )

    if W > 1:
        @pl.when(me + 1 < N)
        def _():
            first_piece().start()

    def send(o, carry):
        query(o).start()
        return carry

    lax.fori_loop(1, N, send, 0)
    for kv in range(KV):
        qin[0, kv] = packed(0, kv)

    load.wait()
    split = one_hot(c == (r % (256 // KV)) * KV + r // (256 // KV))
    per = 256 // KV

    def unmix(b, carry):
        src = pl.ds(pl.multiple_of(b * 256, 256), 256)
        dst = pl.ds(pl.multiple_of(b * per, per), per)
        keys = dot(split, raw[0, src, :]).astype(jnp.bfloat16)
        values = dot(split, raw[1, src, :]).astype(jnp.bfloat16)
        for kv in range(KV):
            kd[kv, :, dst] = jnp.transpose(keys[kv * per:(kv + 1) * per])
            vd[kv, dst, 0:D] = values[kv * per:(kv + 1) * per]
            vd[kv, dst, D:2 * D] = jnp.ones((per, D), jnp.bfloat16)
        return carry

    lax.fori_loop(0, KEYS * KV // 256, unmix, 0)

    def serve(first, count, answers, lines):
        for kv in range(KV):
            rows = [qin[first + i, kv] for i in range(count)]
            s = dot(rows[0] if count == 1 else jnp.concatenate(rows, axis=0), kd[kv])
            top = jnp.max(s, axis=1, keepdims=True)
            p = jnp.exp2((s - top) * (scale * LOG2E)).astype(jnp.bfloat16)
            res = dot(p, vd[kv])
            total = res[:, D:2 * D]
            out = (res[:, 0:D] / total).astype(jnp.bfloat16)
            lse = top * scale + jnp.log(total)
            for i in range(count):
                answers[first + i, kv] = out[i * RP:(i + 1) * RP]
                flat = lse[i * RP:(i + 1) * RP]
                if RL > RP:
                    flat = jnp.concatenate([flat, jnp.zeros((RL - RP, D), jnp.float32)], axis=0)
                lines[first + i, kv:kv + 1, :] = jnp.transpose(flat)[0:1, :]

    def blank(o, carry):
        st[o] = jnp.zeros((2, T * KV, D), jnp.bfloat16)
        return carry

    st[0] = skv_ref[...]
    lax.fori_loop(me + 1, W, blank, 0)
    serve(0, 1, ain, lin)

    def pass_on(o):
        @pl.when(jnp.logical_and(o < W, o <= me))
        def _():
            piece(o - 1).wait_recv()

            @pl.when(jnp.logical_and(o + 1 < W, me + 1 < N))
            def _():
                piece(o).start()

    def turn(first, count):
        for i in range(count):
            pass_on(first + i)
        for i in range(count):
            query(first + i).wait_recv()
        serve(first, count, aout, lout)
        for i in range(count):
            answer(first + i).start()
            answer_lse(first + i).start()

    def two(i, carry):
        turn(1 + 2 * i, 2)
        return carry

    lax.fori_loop(0, (N - 1) // 2, two, 0)
    if (N - 1) % 2:
        turn(N - 1, 1)

    pt = 256 // (T * KV)
    c2 = iota((256, 256), 1)
    r2 = iota((256, 256), 0)
    apart = one_hot(c2 == (r2 % (pt * T)) * KV + r2 // (pt * T))
    for b in range(W // pt):
        keys = dot(apart, st[b * pt:(b + 1) * pt, 0].reshape(256, D)).astype(jnp.bfloat16)
        values = dot(apart, st[b * pt:(b + 1) * pt, 1].reshape(256, D)).astype(jnp.bfloat16)
        for kv in range(KV):
            sk[kv, b * pt * T:(b + 1) * pt * T, :] = keys[kv * pt * T:(kv + 1) * pt * T]
            sv[kv, b * pt * T:(b + 1) * pt * T, 0:D] = values[kv * pt * T:(kv + 1) * pt * T]
            sv[kv, b * pt * T:(b + 1) * pt * T, D:2 * D] = jnp.ones((pt * T, D), jnp.bfloat16)
    row, col = iota((GT, W * T), 0), iota((GT, W * T), 1)
    allowed = jnp.logical_and(col < (me + 1) * T, col <= row % T + jnp.where(col < T, 0, W * T))
    for kv in range(KV):
        s = jnp.where(allowed, dot_nt(qp[kv], sk[kv]), LOW)
        top = jnp.max(s, axis=1, keepdims=True)
        p = jnp.exp2((s - top) * (scale * LOG2E)).astype(jnp.bfloat16)
        res = dot(p, sv[kv])
        m_ref[kv] = jnp.broadcast_to(top * scale, (GT, D))
        l_ref[kv] = res[:, D:2 * D]
        acc[kv] = res[:, 0:D]

    slot = iota((GT, RL), 1).astype(jnp.float32)

    def thirds(x):
        high = x.astype(jnp.bfloat16)
        x = x - high.astype(jnp.float32)
        middle = x.astype(jnp.bfloat16)
        return high, middle, (x - middle.astype(jnp.float32)).astype(jnp.bfloat16)

    def merge(o, carry):
        @pl.when(o > 0)
        def _():
            answer(o).wait_recv()
            answer_lse(o).wait_recv()

        dest = lax.rem(me + o, N)
        column = one_hot(iota((128, RL), 0) == dest)
        for kv in range(KV):
            mine = dot(valt[kv], column)
            hit = one_hot(mine == slot)[:, :RP]
            lines = jnp.broadcast_to(lin[o, kv:kv + 1, :], (D, RL))
            high, middle, low = thirds(jnp.transpose(lines)[:RP])
            got = dot(hit, jnp.concatenate([ain[o, kv], high], axis=1))
            rest = dot(hit, jnp.concatenate([middle, low], axis=1))
            lse = got[:, D:2 * D] + rest[:, 0:D] + rest[:, D:2 * D]
            lse = jnp.where(mine[:, 0:D] >= 0, lse, LOW)
            got = got[:, 0:D]
            new = jnp.maximum(m_ref[kv], lse)
            fade = jnp.exp(m_ref[kv] - new)
            w = jnp.exp(lse - new)
            m_ref[kv] = new
            l_ref[kv] = l_ref[kv] * fade + w
            acc[kv] = acc[kv] * fade + got * w
        return carry

    lax.fori_loop(0, N, merge, 0)

    for kv in range(KV):
        whole = (acc[kv] / l_ref[kv]).astype(jnp.bfloat16)
        for g in range(G):
            fin[:, (kv * G + g) * D:(kv * G + g + 1) * D] = whole[g * T:(g + 1) * T]

    TO = T // KVH
    HD = H * D
    columns = pl.ds(pl.multiple_of(mk * HD, HD), HD)

    def part(j):
        to = lax.rem(mk + j, KVH)
        return pltpu.make_async_remote_copy(
            src_ref=fin.at[pl.ds(pl.multiple_of(to * TO, TO), TO), :], dst_ref=out_ref.at[:, columns],
            send_sem=fs_sem.at[j], recv_sem=fr_sem.at[j], device_id=(me, to), device_id_type=MESH,
        )

    for j in range(1, KVH):
        part(j).start()
    own = pltpu.make_async_copy(
        fin.at[pl.ds(pl.multiple_of(mk * TO, TO), TO), :], out_ref.at[:, columns], load_sem
    )
    own.start()

    def drain(o, carry):
        query(o).wait_send()
        answer(o).wait_send()
        answer_lse(o).wait_send()
        return carry

    lax.fori_loop(1, N, drain, 0)
    if W > 1:
        @pl.when(me + 1 < N)
        def _():
            first_piece().wait_send()

    def drain_piece(o, carry):
        @pl.when(jnp.logical_and(o <= me, me + 1 < N))
        def _():
            piece(o).wait_send()
        return carry

    lax.fori_loop(1, W - 1, drain_piece, 0)
    own.wait()
    for j in range(1, KVH):
        part(j).wait()


def per_device(queries, stretch_kv, cache_kv, selection, block_owner):
    T, H, D = queries.shape
    KV = stretch_kv.shape[2]
    G = H // KV
    top = selection.shape[2]
    N = lax.axis_size("seq")
    KVH = lax.axis_size("kvh")
    C = max(2, top * T // N + 1)
    RP = -(-C * G // 16) * 16
    RL = -(-RP // 128) * 128
    W = min(BLOCK_TOKENS // T, N)
    KEYS = cache_kv.shape[2]
    cfg = (N, KVH, KV, G, T, D, C, RP, RL, W, KEYS)
    bf, f32 = jnp.bfloat16, jnp.float32
    vm = pl.BlockSpec(memory_space=pltpu.VMEM)
    dma = pltpu.SemaphoreType.DMA
    return pl.pallas_call(
        functools.partial(kernel, cfg),
        out_shape=jax.ShapeDtypeStruct((T // KVH, KVH * H * D), bf),
        in_specs=[vm, vm, vm, vm, pl.BlockSpec(memory_space=pl.ANY)],
        out_specs=vm,
        scratch_shapes=[
            pltpu.VMEM((2, KEYS * KV, D), bf),
            pltpu.VMEM((KV, D, KEYS), bf),
            pltpu.VMEM((KV, KEYS, 2 * D), bf),
            pltpu.VMEM((KV, G * T, D), bf),
            pltpu.VMEM((KV, N, G * T), jnp.int32),
            pltpu.VMEM((KV, G * T, 128), bf),
            pltpu.VMEM((N, KV, RP, D), bf),
            pltpu.VMEM((N, KV, RP, D), bf),
            pltpu.VMEM((N, KV, RP, D), bf),
            pltpu.VMEM((N, KV, RP, D), bf),
            pltpu.VMEM((N, 8, RL), f32),
            pltpu.VMEM((N, 8, RL), f32),
            pltpu.VMEM((W, 2, T * KV, D), bf),
            pltpu.VMEM((KV, W * T, D), bf),
            pltpu.VMEM((KV, W * T, 2 * D), bf),
            pltpu.VMEM((KV, G * T, D), f32),
            pltpu.VMEM((KV, G * T, D), f32),
            pltpu.VMEM((KV, G * T, D), f32),
            pltpu.VMEM((T, H * D), bf),
            dma, dma((N,)), dma((N,)), dma((N,)), dma((N,)), dma((N,)), dma((N,)),
            dma((W,)), dma((W,)), dma((KVH,)), dma((KVH,)),
        ],
        compiler_params=pltpu.CompilerParams(
            collective_id=0, has_side_effects=True, vmem_limit_bytes=56 * 1024 * 1024
        ),
        cost_estimate=pl.CostEstimate(
            flops=4 * N * RP * KV * KEYS * D, bytes_accessed=4 * KEYS * KV * D, transcendentals=N * RP * KV * KEYS
        ),
    )(
        selection,
        block_owner.reshape(1, N),
        queries.reshape(T * H, D),
        stretch_kv.reshape(2, T * KV, D),
        cache_kv.reshape(2, KEYS * KV, D),
    )


def solution(mesh):
    placed = (
        P("seq", "kvh", None),
        P(None, "seq", "kvh", None),
        P(None, "seq", None, "kvh", None),
        P("kvh", "seq", None),
        P(),
    )
    return jax.shard_map(
        per_device, mesh=mesh, in_specs=placed, out_specs=P(("seq", "kvh"), None), check_vma=False
    )
```

```python
import functools
import math

import jax
import jax.numpy as jnp
from jax import lax
from jax.experimental import pallas as pl
from jax.experimental.pallas import tpu as pltpu
from jax.sharding import PartitionSpec as P

BLOCK_TOKENS = 2048
MESH = pl.DeviceIdType.MESH
LOW = -1e30
LOG2E = math.log2(math.e)


def iota(shape, axis):
    return lax.broadcasted_iota(jnp.int32, shape, axis)


def dot(a, b):
    return jnp.dot(a, b, preferred_element_type=jnp.float32)


def dot_nt(a, b):
    return lax.dot_general(a, b, (((1,), (1,)), ((), ())), preferred_element_type=jnp.float32)


def one_hot(hit):
    return jnp.where(hit, 1.0, 0.0).astype(jnp.bfloat16)


def kernel(
    cfg,
    sel_ref, owner_ref, q_ref, skv_ref, cache_ref,
    out_ref,
    raw, kd, vd, qp, val, valt, qout, qin, aout, ain, lout, lin, st, sk, sv, m_ref, l_ref, acc, fin,
    load_sem, qs_sem, qr_sem, as_sem, ar_sem, ls_sem, lr_sem, ss_sem, ps_sem, sr_sem, fs_sem, fr_sem,
):
    N, KVH, KV, G, T, D, C, RP, RL, W, KEYS = cfg
    H = KV * G
    GT = G * T
    scale = 1.0 / math.sqrt(D)
    me = lax.axis_index("seq")
    mk = lax.axis_index("kvh")
    load = pltpu.make_async_copy(cache_ref, raw, load_sem)
    load.start()

    barrier = pltpu.get_barrier_semaphore()

    def greet(o, carry):
        pl.semaphore_signal(barrier, inc=1, device_id=(lax.rem(me + o, N), mk), device_id_type=MESH)
        return carry

    lax.fori_loop(1, N, greet, 0)

    def greet_kvh(o, carry):
        pl.semaphore_signal(barrier, inc=1, device_id=(me, lax.rem(mk + o, KVH)), device_id_type=MESH)
        return carry

    lax.fori_loop(1, KVH, greet_kvh, 0)

    tb = 256 // H
    r, c = iota((256, 256), 0), iota((256, 256), 1)
    order = one_hot(c == (r % tb) * H + r // tb)
    for b in range(T // tb):
        moved = dot(order, q_ref[b * 256:(b + 1) * 256, :]).astype(jnp.bfloat16)
        for h in range(H):
            qp[h // G, (h % G) * T + b * tb:(h % G) * T + (b + 1) * tb, :] = moved[h * tb:(h + 1) * tb]

    upper = one_hot(iota((T, T), 0) <= iota((T, T), 1))
    same = one_hot(iota((T, T), 0) == iota((T, T), 1))
    spread = one_hot(iota((T, GT), 0) == iota((T, GT), 1) % T)
    group = iota((N, GT), 1) // T
    owns = one_hot(iota((N, N), 0) == owner_ref[...])
    for kv in range(KV):
        named = iota((T, N), 1) == sel_ref[kv, :, 0:1]
        for k in range(1, sel_ref.shape[2]):
            named = jnp.logical_or(named, iota((T, N), 1) == sel_ref[kv, :, k:k + 1])
        named = dot_nt(owns, one_hot(named)).astype(jnp.bfloat16)
        rank = dot(named, upper) * dot(named, same)
        wide = dot(rank.astype(jnp.bfloat16), spread).astype(jnp.int32)
        rows = jnp.where(wide > 0, (wide - 1) * G + group, -1)
        val[kv] = rows
        padded = rows.astype(jnp.float32)
        if N < 128:
            padded = jnp.concatenate([padded, jnp.zeros((128 - N, GT), jnp.float32)], axis=0)
        valt[kv] = jnp.transpose(padded)

    pl.semaphore_wait(barrier, N - 1 + KVH - 1)

    odd = lax.rem(me, 2)

    def chain(s):
        return pltpu.make_async_remote_copy(
            src_ref=st.at[s], dst_ref=st.at[s + 2], send_sem=ss_sem.at[s], recv_sem=sr_sem.at[s + 2],
            device_id=(lax.rem(me + 2, N), mk), device_id_type=MESH,
        )

    def across(s, step):
        return pltpu.make_async_remote_copy(
            src_ref=st.at[s], dst_ref=st.at[s + step], send_sem=ps_sem.at[s], recv_sem=sr_sem.at[s + step],
            device_id=(lax.rem(me + N + step, N), mk), device_id_type=MESH,
        )

    def pieces_on(s, act):
        @pl.when(jnp.logical_and(s + 2 <= W, me + 2 < N))
        def _():
            act(chain(s))

        @pl.when(jnp.logical_and(odd == 0, s + 1 < W))
        def _():
            act(across(s, 1))

        @pl.when(jnp.logical_and(odd == 1, jnp.logical_and(s >= 2, s - 1 < W)))
        def _():
            act(across(s, -1))

    def query(o):
        return pltpu.make_async_remote_copy(
            src_ref=qout.at[o], dst_ref=qin.at[o], send_sem=qs_sem.at[o],
            recv_sem=qr_sem.at[o], device_id=(lax.rem(me + o, N), mk), device_id_type=MESH,
        )

    def answer(o):
        return pltpu.make_async_remote_copy(
            src_ref=aout.at[o], dst_ref=ain.at[o], send_sem=as_sem.at[o],
            recv_sem=ar_sem.at[o], device_id=(lax.rem(me + N - o, N), mk), device_id_type=MESH,
        )

    def answer_lse(o):
        return pltpu.make_async_remote_copy(
            src_ref=lout.at[o], dst_ref=lin.at[o], send_sem=ls_sem.at[o],
            recv_sem=lr_sem.at[o], device_id=(lax.rem(me + N - o, N), mk), device_id_type=MESH,
        )

    st[0] = skv_ref[...]
    def packed(o, kv):
        line = val[kv, pl.ds(lax.rem(me + o, N), 1), :]
        pick = one_hot(iota((RP, GT), 0) == line)
        return dot(pick, qp[kv]).astype(jnp.bfloat16)

    def send(o, carry):
        for kv in range(KV):
            qout[o, kv] = packed(o, kv)
        query(o).start()
        return carry

    lax.fori_loop(1, N, send, 0)
    pieces_on(0, lambda copy: copy.start())
    for kv in range(KV):
        qin[0, kv] = packed(0, kv)

    load.wait()
    split = one_hot(c == (r % (256 // KV)) * KV + r // (256 // KV))
    per = 256 // KV

    def unmix(b, carry):
        src = pl.ds(pl.multiple_of(b * 256, 256), 256)
        dst = pl.ds(pl.multiple_of(b * per, per), per)
        keys = dot(split, raw[0, src, :]).astype(jnp.bfloat16)
        values = dot(split, raw[1, src, :]).astype(jnp.bfloat16)
        for kv in range(KV):
            kd[kv, dst, :] = keys[kv * per:(kv + 1) * per]
            vd[kv, dst, 0:D] = values[kv * per:(kv + 1) * per]
            vd[kv, dst, D:2 * D] = jnp.ones((per, D), jnp.bfloat16)
        return carry

    lax.fori_loop(0, KEYS * KV // 256, unmix, 0)

    def serve(o, answers, lines):
        for kv in range(KV):
            s = dot_nt(qin[o, kv], kd[kv])
            top = jnp.max(s, axis=1, keepdims=True)
            p = jnp.exp2((s - top) * (scale * LOG2E)).astype(jnp.bfloat16)
            res = dot(p, vd[kv])
            total = res[:, D:2 * D]
            answers[o, kv] = (res[:, 0:D] / total).astype(jnp.bfloat16)
            flat = top * scale + jnp.log(total)
            if RL > RP:
                flat = jnp.concatenate([flat, jnp.zeros((RL - RP, D), jnp.float32)], axis=0)
            lines[o, kv:kv + 1, :] = jnp.transpose(flat)[0:1, :]

    def blank(o, carry):
        st[o] = jnp.zeros((2, T * KV, D), jnp.bfloat16)
        return carry

    lax.fori_loop(me + 1, W, blank, 0)
    serve(0, ain, lin)

    def turn(o, carry):
        query(o).wait_recv()
        serve(o, aout, lout)
        answer(o).start()
        answer_lse(o).start()

        @pl.when(jnp.logical_and(lax.rem(o, 2) == 0, jnp.logical_and(o <= W, o <= me)))
        def _():
            chain(o - 2).wait_recv()
            pieces_on(o, lambda copy: copy.start())

        return carry

    lax.fori_loop(1, N, turn, 0)

    def landed(i, carry):
        @pl.when(2 * i + 1 <= me)
        def _():
            across(2 * i, 1).wait_recv()
        return carry

    lax.fori_loop(0, W // 2, landed, 0)
    pt = 256 // (T * KV)
    c2 = iota((256, 256), 1)
    r2 = iota((256, 256), 0)
    apart = one_hot(c2 == (r2 % (pt * T)) * KV + r2 // (pt * T))
    for b in range(W // pt):
        keys = dot(apart, st[b * pt:(b + 1) * pt, 0].reshape(256, D)).astype(jnp.bfloat16)
        values = dot(apart, st[b * pt:(b + 1) * pt, 1].reshape(256, D)).astype(jnp.bfloat16)
        for kv in range(KV):
            sk[kv, b * pt * T:(b + 1) * pt * T, :] = keys[kv * pt * T:(kv + 1) * pt * T]
            sv[kv, b * pt * T:(b + 1) * pt * T, 0:D] = values[kv * pt * T:(kv + 1) * pt * T]
            sv[kv, b * pt * T:(b + 1) * pt * T, D:2 * D] = jnp.ones((pt * T, D), jnp.bfloat16)
    row, col = iota((GT, W * T), 0), iota((GT, W * T), 1)
    allowed = jnp.logical_and(col < (me + 1) * T, col <= row % T + jnp.where(col < T, 0, W * T))
    for kv in range(KV):
        s = jnp.where(allowed, dot_nt(qp[kv], sk[kv]), LOW)
        top = jnp.max(s, axis=1, keepdims=True)
        p = jnp.exp2((s - top) * (scale * LOG2E)).astype(jnp.bfloat16)
        res = dot(p, sv[kv])
        m_ref[kv] = top * scale
        l_ref[kv] = res[:, D:D + 1]
        acc[kv] = res[:, 0:D]

    lane = iota((GT, 128), 1)
    slot = iota((GT, RL), 1)

    def merge(o, carry):
        @pl.when(o > 0)
        def _():
            answer(o).wait_recv()
            answer_lse(o).wait_recv()

        dest = lax.rem(me + o, N)
        for kv in range(KV):
            mine = jnp.sum(jnp.where(lane == dest, valt[kv], 0.0), axis=1, keepdims=True).astype(jnp.int32)
            hit = slot == mine
            lse = jnp.sum(jnp.where(hit, lin[o, kv:kv + 1, :], 0.0), axis=1, keepdims=True)
            lse = jnp.where(mine >= 0, lse, LOW)
            got = dot(one_hot(hit[:, :RP]), ain[o, kv])
            new = jnp.maximum(m_ref[kv], lse)
            fade = jnp.exp(m_ref[kv] - new)
            w = jnp.exp(lse - new)
            m_ref[kv] = new
            l_ref[kv] = l_ref[kv] * fade + w
            acc[kv] = acc[kv] * fade + got * w
        return carry

    lax.fori_loop(0, N, merge, 0)

    for kv in range(KV):
        whole = (acc[kv] / l_ref[kv]).astype(jnp.bfloat16)
        for g in range(G):
            fin[:, (kv * G + g) * D:(kv * G + g + 1) * D] = whole[g * T:(g + 1) * T]

    TO = T // KVH
    HD = H * D
    columns = pl.ds(pl.multiple_of(mk * HD, HD), HD)

    def part(j):
        to = lax.rem(mk + j, KVH)
        return pltpu.make_async_remote_copy(
            src_ref=fin.at[pl.ds(pl.multiple_of(to * TO, TO), TO), :], dst_ref=out_ref.at[:, columns],
            send_sem=fs_sem.at[j], recv_sem=fr_sem.at[j], device_id=(me, to), device_id_type=MESH,
        )

    for j in range(1, KVH):
        part(j).start()
    own = pltpu.make_async_copy(
        fin.at[pl.ds(pl.multiple_of(mk * TO, TO), TO), :], out_ref.at[:, columns], load_sem
    )
    own.start()

    def drain(o, carry):
        query(o).wait_send()
        answer(o).wait_send()
        answer_lse(o).wait_send()
        return carry

    lax.fori_loop(1, N, drain, 0)

    def drain_piece(i, carry):
        @pl.when(2 * i <= me)
        def _():
            pieces_on(2 * i, lambda copy: copy.wait_send())
        return carry

    lax.fori_loop(0, min(W, N - 1) // 2 + 1, drain_piece, 0)
    own.wait()
    for j in range(1, KVH):
        part(j).wait()


def per_device(queries, stretch_kv, cache_kv, selection, block_owner):
    T, H, D = queries.shape
    KV = stretch_kv.shape[2]
    G = H // KV
    top = selection.shape[2]
    N = lax.axis_size("seq")
    KVH = lax.axis_size("kvh")
    C = max(2, top * T // N + 1)
    RP = -(-C * G // 16) * 16
    RL = -(-RP // 128) * 128
    W = min(BLOCK_TOKENS // T, N)
    KEYS = cache_kv.shape[2]
    cfg = (N, KVH, KV, G, T, D, C, RP, RL, W, KEYS)
    bf, f32 = jnp.bfloat16, jnp.float32
    vm = pl.BlockSpec(memory_space=pltpu.VMEM)
    dma = pltpu.SemaphoreType.DMA
    return pl.pallas_call(
        functools.partial(kernel, cfg),
        out_shape=jax.ShapeDtypeStruct((T // KVH, KVH * H * D), bf),
        in_specs=[vm, vm, vm, vm, pl.BlockSpec(memory_space=pl.ANY)],
        out_specs=vm,
        scratch_shapes=[
            pltpu.VMEM((2, KEYS * KV, D), bf),
            pltpu.VMEM((KV, KEYS, D), bf),
            pltpu.VMEM((KV, KEYS, 2 * D), bf),
            pltpu.VMEM((KV, G * T, D), bf),
            pltpu.VMEM((KV, N, G * T), jnp.int32),
            pltpu.VMEM((KV, G * T, 128), f32),
            pltpu.VMEM((N, KV, RP, D), bf),
            pltpu.VMEM((N, KV, RP, D), bf),
            pltpu.VMEM((N, KV, RP, D), bf),
            pltpu.VMEM((N, KV, RP, D), bf),
            pltpu.VMEM((N, 8, RL), f32),
            pltpu.VMEM((N, 8, RL), f32),
            pltpu.VMEM((W + 2, 2, T * KV, D), bf),
            pltpu.VMEM((KV, W * T, D), bf),
            pltpu.VMEM((KV, W * T, 2 * D), bf),
            pltpu.VMEM((KV, G * T, 1), f32),
            pltpu.VMEM((KV, G * T, 1), f32),
            pltpu.VMEM((KV, G * T, D), f32),
            pltpu.VMEM((T, H * D), bf),
            dma, dma((N,)), dma((N,)), dma((N,)), dma((N,)), dma((N,)), dma((N,)),
            dma((W + 2,)), dma((W + 2,)), dma((W + 2,)), dma((KVH,)), dma((KVH,)),
        ],
        compiler_params=pltpu.CompilerParams(
            collective_id=0, has_side_effects=True, vmem_limit_bytes=56 * 1024 * 1024
        ),
        cost_estimate=pl.CostEstimate(
            flops=4 * N * RP * KV * KEYS * D, bytes_accessed=4 * KEYS * KV * D, transcendentals=N * RP * KV * KEYS
        ),
    )(
        selection,
        block_owner.reshape(1, N),
        queries.reshape(T * H, D),
        stretch_kv.reshape(2, T * KV, D),
        cache_kv.reshape(2, KEYS * KV, D),
    )


def solution(mesh):
    placed = (
        P("seq", "kvh", None),
        P(None, "seq", "kvh", None),
        P(None, "seq", None, "kvh", None),
        P("kvh", "seq", None),
        P(),
    )
    return jax.shard_map(
        per_device, mesh=mesh, in_specs=placed, out_specs=P(("seq", "kvh"), None), check_vma=False
    )
```

```python
import functools
import math

import jax
import jax.numpy as jnp
from jax import lax
from jax.experimental import pallas as pl
from jax.experimental.pallas import tpu as pltpu
from jax.sharding import PartitionSpec as P

BLOCK_TOKENS = 2048
MESH = pl.DeviceIdType.MESH
LOW = -1e30
LOG2E = math.log2(math.e)


def iota(shape, axis):
    return lax.broadcasted_iota(jnp.int32, shape, axis)


def dot(a, b):
    return jnp.dot(a, b, preferred_element_type=jnp.float32)


def dot_nt(a, b):
    return lax.dot_general(a, b, (((1,), (1,)), ((), ())), preferred_element_type=jnp.float32)


def one_hot(hit):
    return jnp.where(hit, 1.0, 0.0).astype(jnp.bfloat16)


def kernel(
    cfg,
    sel_ref, owner_ref, q_ref, skv_ref, cache_ref,
    out_ref,
    raw, kd, vd, qp, val, valt, qout, qin, aout, ain, lout, lin, st, sk, sv, m_ref, l_ref, acc, fin,
    load_sem, qs_sem, qr_sem, as_sem, ar_sem, ls_sem, lr_sem, ss_sem, ps_sem, sr_sem, fs_sem, fr_sem,
):
    N, KVH, KV, G, T, D, C, RP, RL, W, KEYS = cfg
    H = KV * G
    GT = G * T
    scale = 1.0 / math.sqrt(D)
    me = lax.axis_index("seq")
    mk = lax.axis_index("kvh")
    load = pltpu.make_async_copy(cache_ref, raw, load_sem)
    load.start()

    barrier = pltpu.get_barrier_semaphore()

    def greet(o, carry):
        pl.semaphore_signal(barrier, inc=1, device_id=(lax.rem(me + o, N), mk), device_id_type=MESH)
        return carry

    lax.fori_loop(1, N, greet, 0)

    def greet_kvh(o, carry):
        pl.semaphore_signal(barrier, inc=1, device_id=(me, lax.rem(mk + o, KVH)), device_id_type=MESH)
        return carry

    lax.fori_loop(1, KVH, greet_kvh, 0)

    tb = 256 // H
    r, c = iota((256, 256), 0), iota((256, 256), 1)
    order = one_hot(c == (r % tb) * H + r // tb)
    for b in range(T // tb):
        moved = dot(order, q_ref[b * 256:(b + 1) * 256, :]).astype(jnp.bfloat16)
        for h in range(H):
            qp[h // G, (h % G) * T + b * tb:(h % G) * T + (b + 1) * tb, :] = moved[h * tb:(h + 1) * tb]

    upper = one_hot(iota((T, T), 0) <= iota((T, T), 1))
    same = one_hot(iota((T, T), 0) == iota((T, T), 1))
    spread = one_hot(iota((T, GT), 0) == iota((T, GT), 1) % T)
    group = iota((N, GT), 1) // T
    owns = one_hot(iota((N, N), 0) == owner_ref[...])
    for kv in range(KV):
        named = iota((T, N), 1) == sel_ref[kv, :, 0:1]
        for k in range(1, sel_ref.shape[2]):
            named = jnp.logical_or(named, iota((T, N), 1) == sel_ref[kv, :, k:k + 1])
        named = dot_nt(owns, one_hot(named)).astype(jnp.bfloat16)
        rank = dot(named, upper) * dot(named, same)
        wide = dot(rank.astype(jnp.bfloat16), spread).astype(jnp.int32)
        rows = jnp.where(wide > 0, (wide - 1) * G + group, -1)
        val[kv] = rows
        padded = rows.astype(jnp.float32)
        if N < 128:
            padded = jnp.concatenate([padded, jnp.zeros((128 - N, GT), jnp.float32)], axis=0)
        valt[kv] = jnp.transpose(padded)

    pl.semaphore_wait(barrier, N - 1 + KVH - 1)

    odd = lax.rem(me, 2)

    def chain(s):
        return pltpu.make_async_remote_copy(
            src_ref=st.at[s], dst_ref=st.at[s + 2], send_sem=ss_sem.at[s], recv_sem=sr_sem.at[s + 2],
            device_id=(lax.rem(me + 2, N), mk), device_id_type=MESH,
        )

    def across(s, step):
        return pltpu.make_async_remote_copy(
            src_ref=st.at[s], dst_ref=st.at[s + step], send_sem=ps_sem.at[s], recv_sem=sr_sem.at[s + step],
            device_id=(lax.rem(me + N + step, N), mk), device_id_type=MESH,
        )

    def pieces_on(s, act):
        @pl.when(jnp.logical_and(s + 2 <= W, me + 2 < N))
        def _():
            act(chain(s))

        @pl.when(jnp.logical_and(odd == 0, s + 1 < W))
        def _():
            act(across(s, 1))

        @pl.when(jnp.logical_and(odd == 1, jnp.logical_and(s >= 2, s - 1 < W)))
        def _():
            act(across(s, -1))

    def query(o):
        return pltpu.make_async_remote_copy(
            src_ref=qout.at[o], dst_ref=qin.at[o], send_sem=qs_sem.at[o],
            recv_sem=qr_sem.at[o], device_id=(lax.rem(me + o, N), mk), device_id_type=MESH,
        )

    def answer(o):
        return pltpu.make_async_remote_copy(
            src_ref=aout.at[o], dst_ref=ain.at[o], send_sem=as_sem.at[o],
            recv_sem=ar_sem.at[o], device_id=(lax.rem(me + N - o, N), mk), device_id_type=MESH,
        )

    def answer_lse(o):
        return pltpu.make_async_remote_copy(
            src_ref=lout.at[o], dst_ref=lin.at[o], send_sem=ls_sem.at[o],
            recv_sem=lr_sem.at[o], device_id=(lax.rem(me + N - o, N), mk), device_id_type=MESH,
        )

    st[0] = skv_ref[...]
    def packed(o, kv):
        line = val[kv, pl.ds(lax.rem(me + o, N), 1), :]
        pick = one_hot(iota((RP, GT), 0) == line)
        return dot(pick, qp[kv]).astype(jnp.bfloat16)

    def far(i):
        return N // 2 + (i // 2) * (1 - 2 * lax.rem(i, 2))

    def send(i, carry):
        o = far(i)
        for kv in range(KV):
            qout[o, kv] = packed(o, kv)
        query(o).start()
        return carry

    lax.fori_loop(1, N, send, 0)
    pieces_on(0, lambda copy: copy.start())
    for kv in range(KV):
        qin[0, kv] = packed(0, kv)

    load.wait()
    split = one_hot(c == (r % (256 // KV)) * KV + r // (256 // KV))
    per = 256 // KV

    def unmix(b, carry):
        src = pl.ds(pl.multiple_of(b * 256, 256), 256)
        dst = pl.ds(pl.multiple_of(b * per, per), per)
        keys = dot(split, raw[0, src, :]).astype(jnp.bfloat16)
        values = dot(split, raw[1, src, :]).astype(jnp.bfloat16)
        for kv in range(KV):
            kd[kv, dst, :] = keys[kv * per:(kv + 1) * per]
            vd[kv, dst, 0:D] = values[kv * per:(kv + 1) * per]
            vd[kv, dst, D:2 * D] = jnp.ones((per, D), jnp.bfloat16)
        return carry

    lax.fori_loop(0, KEYS * KV // 256, unmix, 0)

    def serve(o, answers, lines):
        for kv in range(KV):
            s = dot_nt(qin[o, kv], kd[kv])
            top = jnp.max(s, axis=1, keepdims=True)
            p = jnp.exp2((s - top) * (scale * LOG2E)).astype(jnp.bfloat16)
            res = dot(p, vd[kv])
            total = res[:, D:2 * D]
            answers[o, kv] = (res[:, 0:D] / total).astype(jnp.bfloat16)
            flat = top * scale + jnp.log(total)
            if RL > RP:
                flat = jnp.concatenate([flat, jnp.zeros((RL - RP, D), jnp.float32)], axis=0)
            lines[o, kv:kv + 1, :] = jnp.transpose(flat)[0:1, :]

    def blank(o, carry):
        st[o] = jnp.zeros((2, T * KV, D), jnp.bfloat16)
        return carry

    lax.fori_loop(me + 1, W, blank, 0)
    serve(0, ain, lin)

    def turn(i, carry):
        o = far(i)
        query(o).wait_recv()
        serve(o, aout, lout)
        answer(o).start()
        answer_lse(o).start()

        @pl.when(jnp.logical_and(lax.rem(i, 2) == 0, jnp.logical_and(i <= W, i <= me)))
        def _():
            chain(i - 2).wait_recv()
            pieces_on(i, lambda copy: copy.start())

        return carry

    lax.fori_loop(1, N, turn, 0)

    def landed(i, carry):
        @pl.when(2 * i + 1 <= me)
        def _():
            across(2 * i, 1).wait_recv()
        return carry

    lax.fori_loop(0, W // 2, landed, 0)
    pt = 256 // (T * KV)
    c2 = iota((256, 256), 1)
    r2 = iota((256, 256), 0)
    apart = one_hot(c2 == (r2 % (pt * T)) * KV + r2 // (pt * T))
    for b in range(W // pt):
        keys = dot(apart, st[b * pt:(b + 1) * pt, 0].reshape(256, D)).astype(jnp.bfloat16)
        values = dot(apart, st[b * pt:(b + 1) * pt, 1].reshape(256, D)).astype(jnp.bfloat16)
        for kv in range(KV):
            sk[kv, b * pt * T:(b + 1) * pt * T, :] = keys[kv * pt * T:(kv + 1) * pt * T]
            sv[kv, b * pt * T:(b + 1) * pt * T, 0:D] = values[kv * pt * T:(kv + 1) * pt * T]
            sv[kv, b * pt * T:(b + 1) * pt * T, D:2 * D] = jnp.ones((pt * T, D), jnp.bfloat16)
    row, col = iota((GT, W * T), 0), iota((GT, W * T), 1)
    allowed = jnp.logical_and(col < (me + 1) * T, col <= row % T + jnp.where(col < T, 0, W * T))
    for kv in range(KV):
        s = jnp.where(allowed, dot_nt(qp[kv], sk[kv]), LOW)
        top = jnp.max(s, axis=1, keepdims=True)
        p = jnp.exp2((s - top) * (scale * LOG2E)).astype(jnp.bfloat16)
        res = dot(p, sv[kv])
        m_ref[kv] = top * scale
        l_ref[kv] = res[:, D:D + 1]
        acc[kv] = res[:, 0:D]

    lane = iota((GT, 128), 1)
    slot = iota((GT, RL), 1)

    def merge(i, carry):
        o = jnp.where(i == 0, 0, far(i))

        @pl.when(o > 0)
        def _():
            answer(o).wait_recv()
            answer_lse(o).wait_recv()

        dest = lax.rem(me + o, N)
        for kv in range(KV):
            mine = jnp.sum(jnp.where(lane == dest, valt[kv], 0.0), axis=1, keepdims=True).astype(jnp.int32)
            hit = slot == mine
            lse = jnp.sum(jnp.where(hit, lin[o, kv:kv + 1, :], 0.0), axis=1, keepdims=True)
            lse = jnp.where(mine >= 0, lse, LOW)
            got = dot(one_hot(hit[:, :RP]), ain[o, kv])
            new = jnp.maximum(m_ref[kv], lse)
            fade = jnp.exp(m_ref[kv] - new)
            w = jnp.exp(lse - new)
            m_ref[kv] = new
            l_ref[kv] = l_ref[kv] * fade + w
            acc[kv] = acc[kv] * fade + got * w
        return carry

    lax.fori_loop(0, N, merge, 0)

    for kv in range(KV):
        whole = (acc[kv] / l_ref[kv]).astype(jnp.bfloat16)
        for g in range(G):
            fin[:, (kv * G + g) * D:(kv * G + g + 1) * D] = whole[g * T:(g + 1) * T]

    TO = T // KVH
    HD = H * D
    columns = pl.ds(pl.multiple_of(mk * HD, HD), HD)

    def part(j):
        to = lax.rem(mk + j, KVH)
        return pltpu.make_async_remote_copy(
            src_ref=fin.at[pl.ds(pl.multiple_of(to * TO, TO), TO), :], dst_ref=out_ref.at[:, columns],
            send_sem=fs_sem.at[j], recv_sem=fr_sem.at[j], device_id=(me, to), device_id_type=MESH,
        )

    for j in range(1, KVH):
        part(j).start()
    own = pltpu.make_async_copy(
        fin.at[pl.ds(pl.multiple_of(mk * TO, TO), TO), :], out_ref.at[:, columns], load_sem
    )
    own.start()

    def drain(o, carry):
        query(o).wait_send()
        answer(o).wait_send()
        answer_lse(o).wait_send()
        return carry

    lax.fori_loop(1, N, drain, 0)

    def drain_piece(i, carry):
        @pl.when(2 * i <= me)
        def _():
            pieces_on(2 * i, lambda copy: copy.wait_send())
        return carry

    lax.fori_loop(0, min(W, N - 1) // 2 + 1, drain_piece, 0)
    own.wait()
    for j in range(1, KVH):
        part(j).wait()


def per_device(queries, stretch_kv, cache_kv, selection, block_owner):
    T, H, D = queries.shape
    KV = stretch_kv.shape[2]
    G = H // KV
    top = selection.shape[2]
    N = lax.axis_size("seq")
    KVH = lax.axis_size("kvh")
    C = max(2, top * T // N + 1)
    RP = -(-C * G // 16) * 16
    RL = -(-RP // 128) * 128
    W = min(BLOCK_TOKENS // T, N)
    KEYS = cache_kv.shape[2]
    cfg = (N, KVH, KV, G, T, D, C, RP, RL, W, KEYS)
    bf, f32 = jnp.bfloat16, jnp.float32
    vm = pl.BlockSpec(memory_space=pltpu.VMEM)
    dma = pltpu.SemaphoreType.DMA
    return pl.pallas_call(
        functools.partial(kernel, cfg),
        out_shape=jax.ShapeDtypeStruct((T // KVH, KVH * H * D), bf),
        in_specs=[vm, vm, vm, vm, pl.BlockSpec(memory_space=pl.ANY)],
        out_specs=vm,
        scratch_shapes=[
            pltpu.VMEM((2, KEYS * KV, D), bf),
            pltpu.VMEM((KV, KEYS, D), bf),
            pltpu.VMEM((KV, KEYS, 2 * D), bf),
            pltpu.VMEM((KV, G * T, D), bf),
            pltpu.VMEM((KV, N, G * T), jnp.int32),
            pltpu.VMEM((KV, G * T, 128), f32),
            pltpu.VMEM((N, KV, RP, D), bf),
            pltpu.VMEM((N, KV, RP, D), bf),
            pltpu.VMEM((N, KV, RP, D), bf),
            pltpu.VMEM((N, KV, RP, D), bf),
            pltpu.VMEM((N, 8, RL), f32),
            pltpu.VMEM((N, 8, RL), f32),
            pltpu.VMEM((W + 2, 2, T * KV, D), bf),
            pltpu.VMEM((KV, W * T, D), bf),
            pltpu.VMEM((KV, W * T, 2 * D), bf),
            pltpu.VMEM((KV, G * T, 1), f32),
            pltpu.VMEM((KV, G * T, 1), f32),
            pltpu.VMEM((KV, G * T, D), f32),
            pltpu.VMEM((T, H * D), bf),
            dma, dma((N,)), dma((N,)), dma((N,)), dma((N,)), dma((N,)), dma((N,)),
            dma((W + 2,)), dma((W + 2,)), dma((W + 2,)), dma((KVH,)), dma((KVH,)),
        ],
        compiler_params=pltpu.CompilerParams(
            collective_id=0, has_side_effects=True, vmem_limit_bytes=56 * 1024 * 1024
        ),
        cost_estimate=pl.CostEstimate(
            flops=4 * N * RP * KV * KEYS * D, bytes_accessed=4 * KEYS * KV * D, transcendentals=N * RP * KV * KEYS
        ),
    )(
        selection,
        block_owner.reshape(1, N),
        queries.reshape(T * H, D),
        stretch_kv.reshape(2, T * KV, D),
        cache_kv.reshape(2, KEYS * KV, D),
    )


def solution(mesh):
    placed = (
        P("seq", "kvh", None),
        P(None, "seq", "kvh", None),
        P(None, "seq", None, "kvh", None),
        P("kvh", "seq", None),
        P(),
    )
    return jax.shard_map(
        per_device, mesh=mesh, in_specs=placed, out_specs=P(("seq", "kvh"), None), check_vma=False
    )
```
